32 devices in a mesh: req: 8 (over z, y), head: 4 (over x, core).
Axes of the slice: x: 2, y: 2, z: 4, core: 2. Of those that a mesh axis runs over, the one named last changes fastest.
Arguments:
- queries: bfloat16 [2048, 8192], P('req', 'head'), may hold values from -8 to 8
- new_keys: bfloat16 [2048, 1024], P('req'), may hold values from -5 to 5
- new_values: bfloat16 [2048, 1024], P('req'), may hold values from -24 to 24
- cache_keys: bfloat16 [16, 256, 1024], P('req'), may hold values from -4 to 4
- cache_values: bfloat16 [16, 256, 1024], P('req'), may hold values from -24 to 24
- request_slot: int32 [8], P('req'), may hold values from 0 to 1
- tenant_ids: int32 [2048], P('req'), may hold values from 0 to 127
- out_weight: bfloat16 [8192, 8192], P('req', 'head'), may hold values from -0.0625 to 0.0625
- adapter_down: bfloat16 [8192, 4096], P('head', 'req'), may hold values from -0.0625 to 0.0625
- adapter_up: bfloat16 [4096, 8192], P('req', 'head'), may hold values from -1 to 1
Outputs:
- mixed: bfloat16 [2048, 8192], P('req', 'head')
The draws below stay inside these ranges and needn't reach their ends.
All inputs are finite; a program needn't handle non-finite values.
Results may differ from the reference program's by a relative error of at most 0.0064.
Values may be sent and summed in bfloat16 or wider, within the bound.
A program may use at most 128 MiB of HBM per device.

```python
import math
import jax
import jax.numpy as jnp
import numpy as np
from jax import lax

D = 8192
HEADS = 64
HD = 128
KVH = 8
RANK = 32
ROWS = 256
REQ_DEV = 2
KEYS = 256
TENANTS = 128
TOKENS = 2048
REQS = 16
N_REQ = 8


def draw_cache_keys(key, part):
    values = jnp.clip(jax.random.normal(jax.random.fold_in(key, 1), (REQS, KEYS, KVH * HD), jnp.float32), -4.0, 4.0)
    return values.astype(jnp.bfloat16)


def draw_queries(key, part):
    values = 1.5 * jnp.clip(jax.random.normal(jax.random.fold_in(key, 3), (TOKENS, HEADS * HD), jnp.float32), -4.0, 4.0)
    return values.astype(jnp.bfloat16)


def place_ends(result, rng, low, largest):
    spot = [jax.random.randint(jax.random.fold_in(rng, axis), (), 0, length) for axis, length in enumerate(result.shape)]
    longest = result.shape.index(max(result.shape))
    next_to = spot[:longest] + [(spot[longest] + 1) % result.shape[longest]] + spot[longest + 1:]
    return result.at[tuple(spot)].set(low).at[tuple(next_to)].set(largest)


def shard_levels(stream_key, shape, pieces, least, largest):
    factor_of, own = 1.0, jax.random.fold_in(stream_key, 6)
    for dim, blocks in pieces:
        draws = jnp.exp(jax.random.uniform(jax.random.fold_in(own, dim), (blocks,), jnp.float32, least / len(pieces), largest / len(pieces)))
        factor_of = factor_of * jnp.repeat(draws, shape[dim] // blocks).reshape([-1 if axis == dim else 1 for axis in range(len(shape))])
    return factor_of


def rank_bounds(number_of, skew):
    portions = [(1 << 20) // math.isqrt(standing ** skew) + 1 for standing in range(1, number_of + 1)]
    width = 1 + sum(portions) // (1 << 30)
    return np.cumsum(np.array([max(1, weight // width) for weight in portions]))


def skewed_ids(stream_key, dims, count, skew):
    listing = rank_bounds(count, skew)
    lot = jax.random.randint(jax.random.fold_in(stream_key, 1), dims, 0, int(listing[count - 1]))
    grade = jnp.searchsorted(jnp.asarray(listing, jnp.int32), lot, side="right")
    return jax.random.permutation(jax.random.fold_in(stream_key, 2), count)[grade].astype(jnp.int32)


def centred(rng, shape, spread, reach, cuts=(), kind=jnp.bfloat16):
    entries = spread * jax.random.normal(rng, shape, jnp.float32)
    if cuts:
        entries = entries * shard_levels(rng, shape, cuts, -0.22, 0.18)
    return jnp.clip(entries, -reach, reach).astype(kind)


def setup_inputs(seed: int = 0) -> dict:
    arg_keys = jax.random.split(jax.random.key(seed), 11)
    return {
        "queries": draw_queries(jax.random.fold_in(arg_keys[10], 71), 0),
        "new_keys": centred(arg_keys[1], (TOKENS, KVH * HD), 1.0, 5.0, ((0, 8),)),
        "new_values": centred(arg_keys[2], (TOKENS, KVH * HD), 4.0, 24.0, ((0, 8),)),
        "cache_keys": draw_cache_keys(jax.random.fold_in(arg_keys[10], 71), 0),
        "cache_values": centred(arg_keys[4], (REQS, KEYS, KVH * HD), 4.0, 24.0, ((0, 8),)),
        "request_slot": place_ends(jax.random.randint(arg_keys[5], (N_REQ,), 0, REQ_DEV), jax.random.fold_in(arg_keys[5], 1), 0, REQ_DEV - 1).astype(jnp.int32),
        "tenant_ids": place_ends(skewed_ids(arg_keys[6], (TOKENS,), TENANTS, 2), jax.random.fold_in(arg_keys[6], 3), 0, TENANTS - 1).astype(jnp.int32),
        "out_weight": centred(arg_keys[7], (D, D), D ** -0.5, 0.0625, ((0, 8), (1, 4))),
        "adapter_down": centred(arg_keys[8], (D, TENANTS * RANK), D ** -0.5, 0.0625, ((0, 4), (1, 8))),
        "adapter_up": centred(arg_keys[9], (TENANTS * RANK, D), RANK ** -0.5, 1.0, ((0, 8), (1, 4))),
    }


def settle(values):
    return lax.optimization_barrier(values.astype(jnp.bfloat16)).astype(jnp.float32)


def widen(block, count):
    group = HEADS // KVH
    return jnp.repeat(block.astype(jnp.float32).reshape(count, KVH, HD), group, axis=1)


def attend(block_queries, keys_old, values_old, keys_new, values_new):
    scale = HD ** -0.5
    queries = block_queries.astype(jnp.float32).reshape(ROWS, HEADS, HD)
    wide_keys_old = widen(keys_old, KEYS)
    wide_values_old = widen(values_old, KEYS)
    wide_keys_new = widen(keys_new, ROWS)
    wide_values_new = widen(values_new, ROWS)
    scores_old = jnp.einsum("qhd,khd->hqk", queries, wide_keys_old) * scale
    scores_new = jnp.einsum("qhd,khd->hqk", queries, wide_keys_new) * scale
    causal = jnp.arange(ROWS, dtype=jnp.int32)[:, None] >= jnp.arange(ROWS, dtype=jnp.int32)[None, :]
    scores_new = jnp.where(causal[None], scores_new, -1.0e30)
    highest = jnp.maximum(jnp.max(scores_old, axis=2), jnp.max(scores_new, axis=2))[:, :, None]
    weights_old = jnp.exp(scores_old - highest)
    weights_new = jnp.where(causal[None], jnp.exp(scores_new - highest), 0.0)
    total = jnp.sum(weights_old, axis=2, keepdims=True) + jnp.sum(weights_new, axis=2, keepdims=True)
    probs_old = settle(weights_old / total)
    probs_new = settle(weights_new / total)
    output = jnp.einsum("hqk,khd->qhd", probs_old, wide_values_old)
    output = output + jnp.einsum("hqk,khd->qhd", probs_new, wide_values_new)
    return output.reshape(ROWS, D).astype(jnp.bfloat16)


def reference(queries, new_keys, new_values, cache_keys, cache_values, request_slot, tenant_ids, out_weight, adapter_down, adapter_up):
    blocks = jnp.arange(N_REQ, dtype=jnp.int32)
    requests = blocks * REQ_DEV + request_slot.astype(jnp.int32)
    down_bank = adapter_down.reshape(D, TENANTS, RANK)
    up_bank = adapter_up.reshape(TENANTS, RANK, D)

    def per_block(index):
        start = (index * ROWS).astype(jnp.int32)
        request = lax.dynamic_index_in_dim(requests, index, 0, keepdims=False)
        attended = attend(
            lax.dynamic_slice_in_dim(queries, start, ROWS, 0),
            lax.dynamic_index_in_dim(cache_keys, request, 0, keepdims=False),
            lax.dynamic_index_in_dim(cache_values, request, 0, keepdims=False),
            lax.dynamic_slice_in_dim(new_keys, start, ROWS, 0),
            lax.dynamic_slice_in_dim(new_values, start, ROWS, 0))
        tenants = lax.dynamic_slice_in_dim(tenant_ids, start, ROWS, 0)
        down = jnp.take(down_bank, tenants, axis=1).astype(jnp.float32)
        shrunk = settle(jnp.einsum("rd,drk->rk", attended.astype(jnp.float32), down))
        lifted = jnp.take(up_bank, tenants, axis=0).astype(jnp.float32)
        delta = jnp.einsum("rk,rkd->rd", shrunk, lifted).astype(jnp.bfloat16)
        return attended, delta

    attended, delta = lax.map(per_block, blocks)
    attended = attended.reshape(TOKENS, D)
    delta = delta.reshape(TOKENS, D)
    base = jnp.dot(attended, out_weight, preferred_element_type=jnp.float32)
    return (base + lax.optimization_barrier(delta).astype(jnp.float32)).astype(jnp.bfloat16)
```

```python
import jax
import jax.numpy as jnp
from jax import lax
from jax.sharding import PartitionSpec as P

HEADS = 64
HD = 128
KVH = 8
RANK = 32


def pick_heads(block, shared_index):
    spread = block.reshape(block.shape[0], KVH, HD)
    return jnp.take(spread, shared_index, axis=1)


def select(tenants, count):
    return tenants[:, None] == jnp.arange(count, dtype=jnp.int32)[None, :]


def reshard_down(weights):
    count = lax.axis_size("req")
    heads = lax.axis_size("head")
    fold = count // heads
    rows = weights.shape[0] // fold
    mine = lax.axis_index("req") % fold
    spread = weights.reshape(fold, rows, weights.shape[1])
    received = []
    for shift in range(fold):
        piece = lax.dynamic_index_in_dim(spread, (mine + shift) % fold, 0, keepdims=False)
        pairs = []
        for source in range(count):
            outer, inner = source // fold, source % fold
            for head in range(heads):
                target = head * fold + (inner + shift) % fold
                pairs.append((source * heads + head, target * heads + outer))
        received.append(lax.ppermute(piece, ("req", "head"), pairs))
    stacked = jnp.stack(received, axis=0)
    order = (mine - jnp.arange(fold, dtype=jnp.int32)) % fold
    stacked = jnp.take(stacked, order, axis=0)
    return jnp.transpose(stacked, (1, 0, 2)).reshape(rows, fold * weights.shape[1])


def gather_features(attended):
    count = lax.axis_size("req")
    heads = lax.axis_size("head")
    quarter = lax.all_to_all(attended, "head", 0, 1, tiled=True)
    part = lax.all_to_all(quarter, "req", 1, 0, tiled=True)
    full = lax.all_gather(part, "head", axis=0, tiled=False)
    rows = attended.shape[0] // heads
    full = full.reshape(heads, count, rows, part.shape[1])
    return jnp.transpose(full, (1, 0, 2, 3)).reshape(count * attended.shape[0], part.shape[1])


def shrink(block, tenants, weights, first):
    count = weights.shape[1] // RANK
    product = jnp.dot(block, weights, preferred_element_type=jnp.float32)
    product = product.reshape(block.shape[0], count, RANK)
    chosen = tenants[:, None] == first + jnp.arange(count, dtype=jnp.int32)[None, :]
    return jnp.sum(jnp.where(chosen[:, :, None], product, 0.0), axis=1)


def spread_tenants(shrunk, tenants, count, first):
    chosen = tenants[:, None] == first + jnp.arange(count, dtype=jnp.int32)[None, :]
    return jnp.where(chosen[:, :, None], shrunk[:, None, :], 0).reshape(
        shrunk.shape[0], count * RANK
    )


def attention(queries, new_keys, new_values, cache_keys, cache_values, request_slot):
    row_count = queries.shape[0]
    local_heads = queries.shape[1] // HD
    group = HEADS // KVH
    shared_index = (
        lax.axis_index("head") * local_heads + jnp.arange(local_heads, dtype=jnp.int32)
    ) // group
    slot_index = request_slot[0]
    keys_old = pick_heads(
        lax.dynamic_index_in_dim(cache_keys, slot_index, 0, keepdims=False), shared_index
    )
    values_old = pick_heads(
        lax.dynamic_index_in_dim(cache_values, slot_index, 0, keepdims=False), shared_index
    )
    keys_new = pick_heads(new_keys, shared_index)
    values_new = pick_heads(new_values, shared_index)
    split_queries = queries.reshape(row_count, local_heads, HD)
    scale = HD ** (-0.5)
    scores_old = (
        jnp.einsum("qhd,khd->hqk", split_queries, keys_old, preferred_element_type=jnp.float32)
        * scale
    )
    scores_new = (
        jnp.einsum("qhd,khd->hqk", split_queries, keys_new, preferred_element_type=jnp.float32)
        * scale
    )
    causal = (
        jnp.arange(row_count, dtype=jnp.int32)[:, None]
        >= jnp.arange(row_count, dtype=jnp.int32)[None, :]
    )
    scores_new = jnp.where(causal[None], scores_new, -1e30)
    highest = jnp.maximum(jnp.max(scores_old, axis=2), jnp.max(scores_new, axis=2))[:, :, None]
    weights_old = jnp.exp(scores_old - highest)
    weights_new = jnp.where(causal[None], jnp.exp(scores_new - highest), 0.0)
    total = jnp.sum(weights_old, axis=2, keepdims=True) + jnp.sum(
        weights_new, axis=2, keepdims=True
    )
    probs_old = (weights_old / total).astype(jnp.bfloat16)
    probs_new = (weights_new / total).astype(jnp.bfloat16)
    output = jnp.einsum("hqk,khd->qhd", probs_old, values_old, preferred_element_type=jnp.float32)
    output = output + jnp.einsum(
        "hqk,khd->qhd", probs_new, values_new, preferred_element_type=jnp.float32
    )
    return output.reshape(row_count, local_heads * HD).astype(jnp.bfloat16)


def local(
    queries,
    new_keys,
    new_values,
    cache_keys,
    cache_values,
    request_slot,
    tenant_ids,
    out_weight,
    adapter_down,
    adapter_up,
):
    down = reshard_down(adapter_down)
    tenants = lax.all_gather(tenant_ids, "req", axis=0, tiled=True)
    attended = attention(queries, new_keys, new_values, cache_keys, cache_values, request_slot)
    block = gather_features(attended)
    down_count = down.shape[1] // RANK
    up_count = adapter_up.shape[0] // RANK
    part = shrink(block, tenants, down, lax.axis_index("head") * down_count)
    shrunk = lax.psum(part, ("req", "head")).astype(jnp.bfloat16)
    spread = spread_tenants(shrunk, tenants, up_count, lax.axis_index("req") * up_count)
    mixed = jnp.dot(block, out_weight, preferred_element_type=jnp.float32)
    mixed = mixed + jnp.dot(spread, adapter_up, preferred_element_type=jnp.float32)
    return lax.psum_scatter(
        mixed.astype(jnp.bfloat16), "req", scatter_dimension=0, tiled=True
    )


def solution(mesh):
    placed = (
        P("req", "head"),
        P("req", None),
        P("req", None),
        P("req", None, None),
        P("req", None, None),
        P("req"),
        P("req"),
        P("req", "head"),
        P("head", "req"),
        P("req", "head"),
    )
    return jax.shard_map(
        local, mesh=mesh, in_specs=placed, out_specs=P("req", "head"), check_vma=False
    )
```

```python
import functools

import jax
import jax.numpy as jnp
from jax import lax
from jax.experimental import pallas as pl
from jax.experimental.pallas import tpu as pltpu
from jax.sharding import PartitionSpec as P

HEADS = 64
HD = 128
KVH = 8
RANK = 32


def pick_heads(block, shared_index):
    spread = block.reshape(block.shape[0], KVH, HD)
    return jnp.take(spread, shared_index, axis=1)


def select(tenants, count):
    return tenants[:, None] == jnp.arange(count, dtype=jnp.int32)[None, :]


def reshard_down(weights):
    count = lax.axis_size("req")
    heads = lax.axis_size("head")
    fold = count // heads
    rows = weights.shape[0] // fold
    mine = lax.axis_index("req") % fold
    spread = weights.reshape(fold, rows, weights.shape[1])
    received = []
    for shift in range(fold):
        piece = lax.dynamic_index_in_dim(spread, (mine + shift) % fold, 0, keepdims=False)
        pairs = []
        for source in range(count):
            outer, inner = source // fold, source % fold
            for head in range(heads):
                target = head * fold + (inner + shift) % fold
                pairs.append((source * heads + head, target * heads + outer))
        received.append(lax.ppermute(piece, ("req", "head"), pairs))
    stacked = jnp.stack(received, axis=0)
    order = (mine - jnp.arange(fold, dtype=jnp.int32)) % fold
    stacked = jnp.take(stacked, order, axis=0)
    return jnp.transpose(stacked, (1, 0, 2)).reshape(rows, fold * weights.shape[1])


def remote(src, dst, send_sem, recv_sem, **axis):
    return pltpu.make_async_remote_copy(
        src_ref=src,
        dst_ref=dst,
        send_sem=send_sem,
        recv_sem=recv_sem,
        device_id=axis,
        device_id_type=pl.DeviceIdType.MESH,
    )


def greet(barrier, **axis):
    pl.semaphore_signal(barrier, inc=1, device_id=axis, device_id_type=pl.DeviceIdType.MESH)


def gather_kernel(count, heads, x_ref, out_ref, send_a, recv_a, local_sem, send_b, recv_b, send_c, recv_c):
    fold = count // heads
    rows = x_ref.shape[0]
    share = rows // heads
    width = out_ref.shape[1]
    peers = heads // 2
    r = lax.axis_index("req")
    h = lax.axis_index("head")
    owner = r // fold
    twin = h + 1 - 2 * (h % 2)
    barrier = pltpu.get_barrier_semaphore()
    for source in range(count):
        @pl.when(jnp.logical_or(r != source, h != owner))
        def _():
            greet(barrier, req=source, head=owner)
    for step in range(1, heads):
        greet(barrier, req=r, head=(h + step) % heads)

    @pl.when(h == owner)
    def _():
        pl.semaphore_wait(barrier, count + heads - 2)

    @pl.when(h != owner)
    def _():
        pl.semaphore_wait(barrier, count + heads - 1)

    def place(source, quarter):
        return out_ref.at[pl.ds(pl.multiple_of(source * rows + quarter * share, share), share), :]

    def first(step):
        target = (step + r) % count
        inner, quarter = target % fold, target // fold
        goal = h * fold + inner
        src = x_ref.at[
            pl.ds(pl.multiple_of(quarter * share, share), share),
            pl.ds(pl.multiple_of(inner * width, width), width),
        ]
        far = jnp.logical_or(goal != r, quarter != h)
        copy = remote(src, place(r, quarter), send_a.at[step], recv_a.at[r], req=goal, head=quarter)
        near = pltpu.make_async_copy(src, place(r, quarter), local_sem)
        return far, copy, near

    for step in range(count):
        far, copy, near = first(step)
        pl.when(far)(copy.start)
        pl.when(jnp.logical_not(far))(near.start)

    def direct(source, kind):
        head = twin if kind == 0 else (h + 2 * kind) % heads
        spot = place(source, h)
        return remote(spot, spot, send_b.at[kind, source], recv_b.at[kind, source], req=r, head=head)

    def forward(source, kind):
        spot = place(source, (h + heads - 2 * kind) % heads)
        return remote(spot, spot, send_c.at[kind, source], recv_c.at[kind, source], req=r, head=twin)

    def pass_on(source):
        for kind in range(1, peers):
            direct(source, kind).wait_recv()
            forward(source, kind).start()

    for step in range(count):
        source = (r + count - step) % count
        spot = place(source, h)
        here = jnp.logical_and(source == r, h == owner)

        @pl.when(here)
        def _():
            pltpu.make_async_copy(spot, spot, local_sem).wait()

        @pl.when(jnp.logical_not(here))
        def _():
            remote(spot, spot, send_a.at[0], recv_a.at[source], req=r, head=twin).wait_recv()

        for kind in [*range(1, peers), 0]:
            direct(source, kind).start()
        if step:
            pass_on((source + 1) % count)
    pass_on((r + 1) % count)
    for step in range(count):
        far, copy, near = first(step)
        pl.when(far)(copy.wait_send)
    for source in range(count):
        direct(source, 0).wait()
        for kind in range(1, peers):
            direct(source, kind).wait_send()
            forward(source, kind).wait()


def gather_features(attended):
    count = lax.axis_size("req")
    heads = lax.axis_size("head")
    width = attended.shape[1] * heads // count
    sems = pltpu.SemaphoreType.DMA
    return pl.pallas_call(
        functools.partial(gather_kernel, count, heads),
        out_shape=jax.ShapeDtypeStruct((count * attended.shape[0], width), attended.dtype),
        in_specs=[pl.BlockSpec(memory_space=pl.ANY)],
        out_specs=pl.BlockSpec(memory_space=pl.ANY),
        scratch_shapes=[
            sems((count,)),
            sems((count,)),
            sems,
            sems((heads // 2, count)),
            sems((heads // 2, count)),
            sems((heads // 2, count)),
            sems((heads // 2, count)),
        ],
        compiler_params=pltpu.CompilerParams(collective_id=0, has_side_effects=True),
    )(attended)


def sum_kernel(count, heads, x_ref, out_ref, from_heads, part, from_reqs, whole, sh, rh, sr, rr, sg, rg, sw, rw):
    r = lax.axis_index("req")
    h = lax.axis_index("head")
    big = part.shape[0]
    small = big // count
    barrier = pltpu.get_barrier_semaphore()
    for step in range(1, heads):
        greet(barrier, req=r, head=(h + step) % heads)
    for step in range(1, count):
        greet(barrier, req=(r + step) % count, head=h)
    pl.semaphore_wait(barrier, heads + count - 2)

    def cut(index, size):
        return pl.ds(pl.multiple_of(index * size, size), size)

    copies = []
    for step in range(1, heads):
        peer = (h + step) % heads
        copies.append(
            remote(x_ref.at[cut(peer, big)], from_heads.at[step], sh.at[step], rh.at[step], req=r, head=peer)
        )
        copies[-1].start()
    total = x_ref[cut(h, big)]
    for step, copy in enumerate(copies):
        copy.wait()
        total = total + from_heads[step + 1]
    part[...] = total
    copies = []
    for step in range(1, count):
        peer = (r + step) % count
        copies.append(
            remote(part.at[cut(peer, small)], from_reqs.at[step], sr.at[step], rr.at[step], req=peer, head=h)
        )
        copies[-1].start()
    total = part[cut(r, small)]
    for step, copy in enumerate(copies):
        copy.wait()
        total = total + from_reqs[step + 1]
    mine = pl.ds(pl.multiple_of(h * big + r * small, small), small)
    whole[mine] = total
    copies = []
    for step in range(1, count):
        peer = (r + step) % count
        copies.append(
            remote(whole.at[mine], whole.at[mine], sg.at[step], rg.at[step], req=peer, head=h)
        )
        copies[-1].start()
    for copy in copies:
        copy.wait()
    copies = []
    for step in range(1, heads):
        peer = (h + step) % heads
        spot = whole.at[cut(h, big)]
        copies.append(remote(spot, spot, sw.at[step], rw.at[step], req=r, head=peer))
        copies[-1].start()
    for copy in copies:
        copy.wait()
    out_ref[...] = whole[...]


def sum_everywhere(part):
    count = lax.axis_size("req")
    heads = lax.axis_size("head")
    groups = 128 // part.shape[1]
    size = part.shape[0] // groups
    packed = jnp.concatenate([part[k * size : (k + 1) * size] for k in range(groups)], axis=1)
    big = size // heads
    sems = pltpu.SemaphoreType.DMA
    total = pl.pallas_call(
        functools.partial(sum_kernel, count, heads),
        out_shape=jax.ShapeDtypeStruct(packed.shape, packed.dtype),
        in_specs=[pl.BlockSpec(memory_space=pltpu.VMEM)],
        out_specs=pl.BlockSpec(memory_space=pltpu.VMEM),
        scratch_shapes=[
            pltpu.VMEM((heads, big, 128), jnp.float32),
            pltpu.VMEM((big, 128), jnp.float32),
            pltpu.VMEM((count, big // count, 128), jnp.float32),
            pltpu.VMEM((size, 128), jnp.float32),
            sems((heads,)),
            sems((heads,)),
            sems((count,)),
            sems((count,)),
            sems((count,)),
            sems((count,)),
            sems((heads,)),
            sems((heads,)),
        ],
        compiler_params=pltpu.CompilerParams(collective_id=1, has_side_effects=True),
    )(packed)
    width = part.shape[1]
    return jnp.concatenate(
        [total[:, k * width : (k + 1) * width] for k in range(groups)], axis=0
    )


def scatter_kernel(outer, chunks, a_ref, w_ref, s_ref, u_ref, out_ref, given, taken, kept, up, down,
                   send_p, recv_p, send_l, recv_u, recv_d):
    rows, cols = out_ref.shape
    width = cols // chunks
    r = lax.axis_index("req")
    a, b = r // 2, r % 2
    barrier = pltpu.get_barrier_semaphore()
    greet(barrier, req=2 * a + 1 - b)

    @pl.when(a > 0)
    def _():
        greet(barrier, req=r - 2)

    @pl.when(a < outer - 1)
    def _():
        greet(barrier, req=r + 2)

    inside = jnp.logical_and(a > 0, a < outer - 1)

    @pl.when(inside)
    def _():
        pl.semaphore_wait(barrier, 3)

    @pl.when(jnp.logical_not(inside))
    def _():
        pl.semaphore_wait(barrier, 2)

    def goal(step):
        result = a
        for place in range(outer):
            order = sorted(range(outer), key=lambda t: (-abs(t - place), t))
            for at in range(outer):
                result = jnp.where(jnp.logical_and(a == place, step == at), order[at], result)
        return result

    def product(target, inner, chunk):
        block = pl.ds(pl.multiple_of((target * 2 + inner) * rows, rows), rows)
        span = pl.ds(pl.multiple_of(chunk * width, width), width)
        value = jnp.dot(a_ref[block, :], w_ref[:, span], preferred_element_type=jnp.float32)
        return value + jnp.dot(s_ref[block, :], u_ref[:, span], preferred_element_type=jnp.float32)

    def pair(target, chunk):
        return remote(
            given.at[target, chunk], taken.at[target, chunk], send_p.at[target, chunk],
            recv_p.at[target, chunk], req=2 * a + 1 - b,
        )

    def higher(target, chunk):
        return remote(
            kept.at[target, chunk], up.at[target, chunk], send_l.at[target, chunk],
            recv_u.at[target, chunk], req=r + 2,
        )

    def lower(target, chunk):
        return remote(
            kept.at[target, chunk], down.at[target, chunk], send_l.at[target, chunk],
            recv_d.at[target, chunk], req=r - 2,
        )

    def give(unit, carry):
        target, chunk = goal(unit // chunks), unit % chunks
        given[target, chunk] = product(target, 1 - b, chunk).astype(given.dtype)
        pair(target, chunk).start()
        return carry

    lax.fori_loop(0, outer * chunks, give, 0)

    def reduce(unit, carry):
        target, chunk = goal(unit // chunks), unit % chunks
        value = product(target, b, chunk)
        pair(target, chunk).wait_recv()
        value = value + taken[target, chunk].astype(jnp.float32)

        @pl.when(jnp.logical_and(target > a, a == 0))
        def _():
            kept[target, chunk] = value.astype(kept.dtype)

        @pl.when(jnp.logical_and(target > a, a > 0))
        def _():
            higher(target, chunk).wait_recv()
            kept[target, chunk] = (value + up[target, chunk].astype(jnp.float32)).astype(kept.dtype)

        @pl.when(target > a)
        def _():
            higher(target, chunk).start()

        @pl.when(jnp.logical_and(target < a, a == outer - 1))
        def _():
            kept[target, chunk] = value.astype(kept.dtype)

        @pl.when(jnp.logical_and(target < a, a < outer - 1))
        def _():
            lower(target, chunk).wait_recv()
            kept[target, chunk] = (value + down[target, chunk].astype(jnp.float32)).astype(kept.dtype)

        @pl.when(target < a)
        def _():
            lower(target, chunk).start()

        span = pl.ds(pl.multiple_of(chunk * width, width), width)

        @pl.when(jnp.logical_and(target == a, a == 0))
        def _():
            lower(target, chunk).wait_recv()
            out_ref[:, span] = (value + down[target, chunk].astype(jnp.float32)).astype(out_ref.dtype)

        @pl.when(jnp.logical_and(target == a, a == outer - 1))
        def _():
            higher(target, chunk).wait_recv()
            out_ref[:, span] = (value + up[target, chunk].astype(jnp.float32)).astype(out_ref.dtype)

        @pl.when(jnp.logical_and(target == a, jnp.logical_and(a > 0, a < outer - 1)))
        def _():
            higher(target, chunk).wait_recv()
            lower(target, chunk).wait_recv()
            both = up[target, chunk].astype(jnp.float32) + down[target, chunk].astype(jnp.float32)
            out_ref[:, span] = (value + both).astype(out_ref.dtype)

        return carry

    lax.fori_loop(0, outer * chunks, reduce, 0)

    def finish(unit, carry):
        target, chunk = unit // chunks, unit % chunks
        pair(target, chunk).wait_send()
        pl.when(target > a)(higher(target, chunk).wait_send)
        pl.when(target < a)(lower(target, chunk).wait_send)
        return carry

    lax.fori_loop(0, outer * chunks, finish, 0)


def scatter_products(block, weights, spread, lifts):
    count = lax.axis_size("req")
    outer = count // 2
    chunks = 4
    rows = block.shape[0] // count
    cols = weights.shape[1]
    slots = pltpu.VMEM((outer, chunks, rows, cols // chunks), jnp.bfloat16)
    sems = pltpu.SemaphoreType.DMA((outer, chunks))
    return pl.pallas_call(
        functools.partial(scatter_kernel, outer, chunks),
        out_shape=jax.ShapeDtypeStruct((rows, cols), jnp.bfloat16),
        in_specs=[pl.BlockSpec(memory_space=pltpu.VMEM)] * 4,
        out_specs=pl.BlockSpec(memory_space=pltpu.VMEM),
        scratch_shapes=[slots] * 5 + [sems] * 5,
        compiler_params=pltpu.CompilerParams(
            collective_id=2, has_side_effects=True, vmem_limit_bytes=52 * 1024 * 1024
        ),
    )(block, weights, spread, lifts)


def shrink(block, tenants, weights, first):
    count = weights.shape[1] // RANK
    product = jnp.dot(block, weights, preferred_element_type=jnp.float32)
    product = product.reshape(block.shape[0], count, RANK)
    chosen = tenants[:, None] == first + jnp.arange(count, dtype=jnp.int32)[None, :]
    return jnp.sum(jnp.where(chosen[:, :, None], product, 0.0), axis=1)


def spread_tenants(shrunk, tenants, count, first):
    chosen = tenants[:, None] == first + jnp.arange(count, dtype=jnp.int32)[None, :]
    return jnp.where(chosen[:, :, None], shrunk[:, None, :], 0).reshape(
        shrunk.shape[0], count * RANK
    )


def attention(queries, new_keys, new_values, cache_keys, cache_values, request_slot):
    row_count = queries.shape[0]
    local_heads = queries.shape[1] // HD
    group = HEADS // KVH
    shared_index = (
        lax.axis_index("head") * local_heads + jnp.arange(local_heads, dtype=jnp.int32)
    ) // group
    slot_index = request_slot[0]
    keys_old = pick_heads(
        lax.dynamic_index_in_dim(cache_keys, slot_index, 0, keepdims=False), shared_index
    )
    values_old = pick_heads(
        lax.dynamic_index_in_dim(cache_values, slot_index, 0, keepdims=False), shared_index
    )
    keys_new = pick_heads(new_keys, shared_index)
    values_new = pick_heads(new_values, shared_index)
    split_queries = queries.reshape(row_count, local_heads, HD)
    scale = HD ** (-0.5)
    scores_old = (
        jnp.einsum("qhd,khd->hqk", split_queries, keys_old, preferred_element_type=jnp.float32)
        * scale
    )
    scores_new = (
        jnp.einsum("qhd,khd->hqk", split_queries, keys_new, preferred_element_type=jnp.float32)
        * scale
    )
    causal = (
        jnp.arange(row_count, dtype=jnp.int32)[:, None]
        >= jnp.arange(row_count, dtype=jnp.int32)[None, :]
    )
    scores_new = jnp.where(causal[None], scores_new, -1e30)
    highest = jnp.maximum(jnp.max(scores_old, axis=2), jnp.max(scores_new, axis=2))[:, :, None]
    weights_old = jnp.exp(scores_old - highest)
    weights_new = jnp.where(causal[None], jnp.exp(scores_new - highest), 0.0)
    total = jnp.sum(weights_old, axis=2, keepdims=True) + jnp.sum(
        weights_new, axis=2, keepdims=True
    )
    probs_old = (weights_old / total).astype(jnp.bfloat16)
    probs_new = (weights_new / total).astype(jnp.bfloat16)
    output = jnp.einsum("hqk,khd->qhd", probs_old, values_old, preferred_element_type=jnp.float32)
    output = output + jnp.einsum(
        "hqk,khd->qhd", probs_new, values_new, preferred_element_type=jnp.float32
    )
    return output.reshape(row_count, local_heads * HD).astype(jnp.bfloat16)


def local(
    queries,
    new_keys,
    new_values,
    cache_keys,
    cache_values,
    request_slot,
    tenant_ids,
    out_weight,
    adapter_down,
    adapter_up,
):
    down = reshard_down(adapter_down)
    tenants = lax.all_gather(tenant_ids, "req", axis=0, tiled=True)
    attended = attention(queries, new_keys, new_values, cache_keys, cache_values, request_slot)
    block = gather_features(attended)
    down_count = down.shape[1] // RANK
    up_count = adapter_up.shape[0] // RANK
    part = shrink(block, tenants, down, lax.axis_index("head") * down_count)
    shrunk = sum_everywhere(part).astype(jnp.bfloat16)
    spread = spread_tenants(shrunk, tenants, up_count, lax.axis_index("req") * up_count)
    return scatter_products(block, out_weight, spread, adapter_up)


def solution(mesh):
    placed = (
        P("req", "head"),
        P("req", None),
        P("req", None),
        P("req", None, None),
        P("req", None, None),
        P("req"),
        P("req"),
        P("req", "head"),
        P("head", "req"),
        P("req", "head"),
    )
    return jax.shard_map(
        local, mesh=mesh, in_specs=placed, out_specs=P("req", "head"), check_vma=False
    )
```

```python
import functools

import jax
import jax.numpy as jnp
from jax import lax
from jax.experimental import pallas as pl
from jax.experimental.pallas import tpu as pltpu
from jax.sharding import PartitionSpec as P

HEADS = 64
HD = 128
KVH = 8
RANK = 32


def pick_heads(block, shared_index):
    spread = block.reshape(block.shape[0], KVH, HD)
    return jnp.take(spread, shared_index, axis=1)


def select(tenants, count):
    return tenants[:, None] == jnp.arange(count, dtype=jnp.int32)[None, :]


def reshard_down(weights):
    count = lax.axis_size("req")
    heads = lax.axis_size("head")
    fold = count // heads
    rows = weights.shape[0] // fold
    mine = lax.axis_index("req") % fold
    spread = weights.reshape(fold, rows, weights.shape[1])
    received = []
    for shift in range(fold):
        piece = lax.dynamic_index_in_dim(spread, (mine + shift) % fold, 0, keepdims=False)
        pairs = []
        for source in range(count):
            outer, inner = source // fold, source % fold
            for head in range(heads):
                target = head * fold + (inner + shift) % fold
                pairs.append((source * heads + head, target * heads + outer))
        received.append(lax.ppermute(piece, ("req", "head"), pairs))
    stacked = jnp.stack(received, axis=0)
    order = (mine - jnp.arange(fold, dtype=jnp.int32)) % fold
    stacked = jnp.take(stacked, order, axis=0)
    return jnp.transpose(stacked, (1, 0, 2)).reshape(rows, fold * weights.shape[1])


def remote(src, dst, send_sem, recv_sem, **axis):
    return pltpu.make_async_remote_copy(
        src_ref=src,
        dst_ref=dst,
        send_sem=send_sem,
        recv_sem=recv_sem,
        device_id=axis,
        device_id_type=pl.DeviceIdType.MESH,
    )


def greet(barrier, **axis):
    pl.semaphore_signal(barrier, inc=1, device_id=axis, device_id_type=pl.DeviceIdType.MESH)


def gather_kernel(count, heads, x_ref, ids_ref, out_ref, all_ref, send_t, recv_t, send_a, recv_a, local_sem, send_b, recv_b, send_c, recv_c):
    fold = count // heads
    rows = x_ref.shape[0]
    share = rows // heads
    width = out_ref.shape[1]
    peers = heads // 2
    r = lax.axis_index("req")
    h = lax.axis_index("head")
    owner = r // fold
    twin = h + 1 - 2 * (h % 2)
    barrier = pltpu.get_barrier_semaphore()
    for source in range(count):
        @pl.when(jnp.logical_or(r != source, h != owner))
        def _():
            greet(barrier, req=source, head=owner)
    for step in range(1, heads):
        greet(barrier, req=r, head=(h + step) % heads)

    for step in range(1, count):
        greet(barrier, req=(r + step) % count, head=h)

    @pl.when(h == owner)
    def _():
        pl.semaphore_wait(barrier, 2 * count + heads - 3)

    @pl.when(h != owner)
    def _():
        pl.semaphore_wait(barrier, 2 * count + heads - 2)

    def place(source, quarter):
        return out_ref.at[pl.ds(pl.multiple_of(source * rows + quarter * share, share), share), :]

    def first(step):
        target = (step + r) % count
        inner, quarter = target % fold, target // fold
        goal = h * fold + inner
        src = x_ref.at[
            pl.ds(pl.multiple_of(quarter * share, share), share),
            pl.ds(pl.multiple_of(inner * width, width), width),
        ]
        far = jnp.logical_or(goal != r, quarter != h)
        copy = remote(src, place(r, quarter), send_a.at[step], recv_a.at[r], req=goal, head=quarter)
        near = pltpu.make_async_copy(src, place(r, quarter), local_sem)
        return far, copy, near

    for step in range(count):
        far, copy, near = first(step)
        pl.when(far)(copy.start)
        pl.when(jnp.logical_not(far))(near.start)

    ids = []
    for step in range(1, count):
        ids.append(
            remote(
                ids_ref, all_ref.at[r], send_t.at[step], recv_t.at[step], req=(r + step) % count, head=h
            )
        )
        ids[-1].start()
    all_ref[r] = ids_ref[...]

    def direct(source, kind):
        head = twin if kind == 0 else (h + 2 * kind) % heads
        spot = place(source, h)
        return remote(spot, spot, send_b.at[kind, source], recv_b.at[kind, source], req=r, head=head)

    def forward(source, kind):
        spot = place(source, (h + heads - 2 * kind) % heads)
        return remote(spot, spot, send_c.at[kind, source], recv_c.at[kind, source], req=r, head=twin)

    def pass_on(source):
        for kind in range(1, peers):
            direct(source, kind).wait_recv()
            forward(source, kind).start()

    for step in range(count):
        source = (r + count - step) % count
        spot = place(source, h)
        here = jnp.logical_and(source == r, h == owner)

        @pl.when(here)
        def _():
            pltpu.make_async_copy(spot, spot, local_sem).wait()

        @pl.when(jnp.logical_not(here))
        def _():
            remote(spot, spot, send_a.at[0], recv_a.at[source], req=r, head=twin).wait_recv()

        for kind in [*range(1, peers), 0]:
            direct(source, kind).start()
        if step:
            pass_on((source + 1) % count)
    pass_on((r + 1) % count)
    for copy in ids:
        copy.wait()
    for step in range(count):
        far, copy, near = first(step)
        pl.when(far)(copy.wait_send)
    for source in range(count):
        direct(source, 0).wait()
        for kind in range(1, peers):
            direct(source, kind).wait_send()
            forward(source, kind).wait()


def gather_features(attended, tenant_ids):
    count = lax.axis_size("req")
    heads = lax.axis_size("head")
    width = attended.shape[1] * heads // count
    sems = pltpu.SemaphoreType.DMA
    ids = tenant_ids.reshape(-1, 128)
    block, tenants = pl.pallas_call(
        functools.partial(gather_kernel, count, heads),
        out_shape=(
            jax.ShapeDtypeStruct((count * attended.shape[0], width), attended.dtype),
            jax.ShapeDtypeStruct((count, *ids.shape), ids.dtype),
        ),
        in_specs=[pl.BlockSpec(memory_space=pltpu.VMEM)] * 2,
        out_specs=(pl.BlockSpec(memory_space=pltpu.VMEM),) * 2,
        scratch_shapes=[
            sems((count,)),
            sems((count,)),
            sems((count,)),
            sems((count,)),
            sems,
            sems((heads // 2, count)),
            sems((heads // 2, count)),
            sems((heads // 2, count)),
            sems((heads // 2, count)),
        ],
        compiler_params=pltpu.CompilerParams(
            collective_id=0, has_side_effects=True, vmem_limit_bytes=32 * 1024 * 1024
        ),
    )(attended, ids)
    return block, tenants.reshape(-1)


def sum_kernel(count, heads, x_ref, out_ref, from_heads, part, from_reqs, whole, sh, rh, sr, rr, sg, rg, sw, rw):
    r = lax.axis_index("req")
    h = lax.axis_index("head")
    big = part.shape[0]
    small = big // count
    barrier = pltpu.get_barrier_semaphore()
    for step in range(1, heads):
        greet(barrier, req=r, head=(h + step) % heads)
    for step in range(1, count):
        greet(barrier, req=(r + step) % count, head=h)
    pl.semaphore_wait(barrier, heads + count - 2)

    def cut(index, size):
        return pl.ds(pl.multiple_of(index * size, size), size)

    copies = []
    for step in range(1, heads):
        peer = (h + step) % heads
        copies.append(
            remote(x_ref.at[cut(peer, big)], from_heads.at[step], sh.at[step], rh.at[step], req=r, head=peer)
        )
        copies[-1].start()
    total = x_ref[cut(h, big)]
    for step, copy in enumerate(copies):
        copy.wait()
        total = total + from_heads[step + 1]
    part[...] = total
    copies = []
    for step in range(1, count):
        peer = (r + step) % count
        copies.append(
            remote(part.at[cut(peer, small)], from_reqs.at[step], sr.at[step], rr.at[step], req=peer, head=h)
        )
        copies[-1].start()
    total = part[cut(r, small)]
    for step, copy in enumerate(copies):
        copy.wait()
        total = total + from_reqs[step + 1]
    mine = pl.ds(pl.multiple_of(h * big + r * small, small), small)
    whole[mine] = total
    copies = []
    for step in range(1, count):
        peer = (r + step) % count
        copies.append(
            remote(whole.at[mine], whole.at[mine], sg.at[step], rg.at[step], req=peer, head=h)
        )
        copies[-1].start()
    for copy in copies:
        copy.wait()
    copies = []
    for step in range(1, heads):
        peer = (h + step) % heads
        spot = whole.at[cut(h, big)]
        copies.append(remote(spot, spot, sw.at[step], rw.at[step], req=r, head=peer))
        copies[-1].start()
    for copy in copies:
        copy.wait()
    out_ref[...] = whole[...]


def sum_everywhere(part):
    count = lax.axis_size("req")
    heads = lax.axis_size("head")
    groups = 128 // part.shape[1]
    size = part.shape[0] // groups
    packed = jnp.concatenate([part[k * size : (k + 1) * size] for k in range(groups)], axis=1)
    big = size // heads
    sems = pltpu.SemaphoreType.DMA
    total = pl.pallas_call(
        functools.partial(sum_kernel, count, heads),
        out_shape=jax.ShapeDtypeStruct(packed.shape, packed.dtype),
        in_specs=[pl.BlockSpec(memory_space=pltpu.VMEM)],
        out_specs=pl.BlockSpec(memory_space=pltpu.VMEM),
        scratch_shapes=[
            pltpu.VMEM((heads, big, 128), jnp.float32),
            pltpu.VMEM((big, 128), jnp.float32),
            pltpu.VMEM((count, big // count, 128), jnp.float32),
            pltpu.VMEM((size, 128), jnp.float32),
            sems((heads,)),
            sems((heads,)),
            sems((count,)),
            sems((count,)),
            sems((count,)),
            sems((count,)),
            sems((heads,)),
            sems((heads,)),
        ],
        compiler_params=pltpu.CompilerParams(collective_id=1, has_side_effects=True),
    )(packed)
    width = part.shape[1]
    return jnp.concatenate(
        [total[:, k * width : (k + 1) * width] for k in range(groups)], axis=0
    )


def scatter_kernel(outer, chunks, a_ref, w_ref, s_ref, u_ref, out_ref, given, taken, kept, up, down,
                   send_p, recv_p, send_l, recv_u, recv_d):
    rows, cols = out_ref.shape
    width = cols // chunks
    r = lax.axis_index("req")
    a, b = r // 2, r % 2
    barrier = pltpu.get_barrier_semaphore()
    greet(barrier, req=2 * a + 1 - b)

    @pl.when(a > 0)
    def _():
        greet(barrier, req=r - 2)

    @pl.when(a < outer - 1)
    def _():
        greet(barrier, req=r + 2)

    inside = jnp.logical_and(a > 0, a < outer - 1)

    @pl.when(inside)
    def _():
        pl.semaphore_wait(barrier, 3)

    @pl.when(jnp.logical_not(inside))
    def _():
        pl.semaphore_wait(barrier, 2)

    def goal(step):
        result = a
        for place in range(outer):
            order = sorted(range(outer), key=lambda t: (-abs(t - place), t))
            for at in range(outer):
                result = jnp.where(jnp.logical_and(a == place, step == at), order[at], result)
        return result

    def product(target, inner, chunk):
        block = pl.ds(pl.multiple_of((target * 2 + inner) * rows, rows), rows)
        span = pl.ds(pl.multiple_of(chunk * width, width), width)
        value = jnp.dot(a_ref[block, :], w_ref[:, span], preferred_element_type=jnp.float32)
        return value + jnp.dot(s_ref[block, :], u_ref[:, span], preferred_element_type=jnp.float32)

    def pair(target, chunk):
        return remote(
            given.at[target, chunk], taken.at[target, chunk], send_p.at[target, chunk],
            recv_p.at[target, chunk], req=2 * a + 1 - b,
        )

    def higher(target, chunk):
        return remote(
            kept.at[target, chunk], up.at[target, chunk], send_l.at[target, chunk],
            recv_u.at[target, chunk], req=r + 2,
        )

    def lower(target, chunk):
        return remote(
            kept.at[target, chunk], down.at[target, chunk], send_l.at[target, chunk],
            recv_d.at[target, chunk], req=r - 2,
        )

    def give(unit, carry):
        target, chunk = goal(unit // chunks), unit % chunks
        given[target, chunk] = product(target, 1 - b, chunk).astype(given.dtype)
        pair(target, chunk).start()
        return carry

    lax.fori_loop(0, outer * chunks, give, 0)

    def reduce(unit, carry):
        target, chunk = goal(unit // chunks), unit % chunks
        value = product(target, b, chunk)
        pair(target, chunk).wait_recv()
        value = value + taken[target, chunk].astype(jnp.float32)

        @pl.when(jnp.logical_and(target > a, a == 0))
        def _():
            kept[target, chunk] = value.astype(kept.dtype)

        @pl.when(jnp.logical_and(target > a, a > 0))
        def _():
            higher(target, chunk).wait_recv()
            kept[target, chunk] = (value + up[target, chunk].astype(jnp.float32)).astype(kept.dtype)

        @pl.when(target > a)
        def _():
            higher(target, chunk).start()

        @pl.when(jnp.logical_and(target < a, a == outer - 1))
        def _():
            kept[target, chunk] = value.astype(kept.dtype)

        @pl.when(jnp.logical_and(target < a, a < outer - 1))
        def _():
            lower(target, chunk).wait_recv()
            kept[target, chunk] = (value + down[target, chunk].astype(jnp.float32)).astype(kept.dtype)

        @pl.when(target < a)
        def _():
            lower(target, chunk).start()

        span = pl.ds(pl.multiple_of(chunk * width, width), width)

        @pl.when(jnp.logical_and(target == a, a == 0))
        def _():
            lower(target, chunk).wait_recv()
            out_ref[:, span] = (value + down[target, chunk].astype(jnp.float32)).astype(out_ref.dtype)

        @pl.when(jnp.logical_and(target == a, a == outer - 1))
        def _():
            higher(target, chunk).wait_recv()
            out_ref[:, span] = (value + up[target, chunk].astype(jnp.float32)).astype(out_ref.dtype)

        @pl.when(jnp.logical_and(target == a, jnp.logical_and(a > 0, a < outer - 1)))
        def _():
            higher(target, chunk).wait_recv()
            lower(target, chunk).wait_recv()
            both = up[target, chunk].astype(jnp.float32) + down[target, chunk].astype(jnp.float32)
            out_ref[:, span] = (value + both).astype(out_ref.dtype)

        return carry

    lax.fori_loop(0, outer * chunks, reduce, 0)

    def finish(unit, carry):
        target, chunk = unit // chunks, unit % chunks
        pair(target, chunk).wait_send()
        pl.when(target > a)(higher(target, chunk).wait_send)
        pl.when(target < a)(lower(target, chunk).wait_send)
        return carry

    lax.fori_loop(0, outer * chunks, finish, 0)


def scatter_products(block, weights, spread, lifts):
    count = lax.axis_size("req")
    outer = count // 2
    chunks = 4
    rows = block.shape[0] // count
    cols = weights.shape[1]
    slots = pltpu.VMEM((outer, chunks, rows, cols // chunks), jnp.bfloat16)
    sems = pltpu.SemaphoreType.DMA((outer, chunks))
    return pl.pallas_call(
        functools.partial(scatter_kernel, outer, chunks),
        out_shape=jax.ShapeDtypeStruct((rows, cols), jnp.bfloat16),
        in_specs=[pl.BlockSpec(memory_space=pltpu.VMEM)] * 4,
        out_specs=pl.BlockSpec(memory_space=pltpu.VMEM),
        scratch_shapes=[slots] * 5 + [sems] * 5,
        compiler_params=pltpu.CompilerParams(
            collective_id=2, has_side_effects=True, vmem_limit_bytes=52 * 1024 * 1024
        ),
    )(block, weights, spread, lifts)


def shrink(block, tenants, weights, first):
    count = weights.shape[1] // RANK
    product = jnp.dot(block, weights, preferred_element_type=jnp.float32)
    product = product.reshape(block.shape[0], count, RANK)
    chosen = tenants[:, None] == first + jnp.arange(count, dtype=jnp.int32)[None, :]
    return jnp.sum(jnp.where(chosen[:, :, None], product, 0.0), axis=1)


def spread_tenants(shrunk, tenants, count, first):
    chosen = tenants[:, None] == first + jnp.arange(count, dtype=jnp.int32)[None, :]
    return jnp.where(chosen[:, :, None], shrunk[:, None, :], 0).reshape(
        shrunk.shape[0], count * RANK
    )


def attention(queries, new_keys, new_values, cache_keys, cache_values, request_slot):
    row_count = queries.shape[0]
    local_heads = queries.shape[1] // HD
    group = HEADS // KVH
    shared_index = (
        lax.axis_index("head") * local_heads + jnp.arange(local_heads, dtype=jnp.int32)
    ) // group
    slot_index = request_slot[0]
    keys_old = pick_heads(
        lax.dynamic_index_in_dim(cache_keys, slot_index, 0, keepdims=False), shared_index
    )
    values_old = pick_heads(
        lax.dynamic_index_in_dim(cache_values, slot_index, 0, keepdims=False), shared_index
    )
    keys_new = pick_heads(new_keys, shared_index)
    values_new = pick_heads(new_values, shared_index)
    split_queries = queries.reshape(row_count, local_heads, HD)
    scale = HD ** (-0.5)
    scores_old = (
        jnp.einsum("qhd,khd->hqk", split_queries, keys_old, preferred_element_type=jnp.float32)
        * scale
    )
    scores_new = (
        jnp.einsum("qhd,khd->hqk", split_queries, keys_new, preferred_element_type=jnp.float32)
        * scale
    )
    causal = (
        jnp.arange(row_count, dtype=jnp.int32)[:, None]
        >= jnp.arange(row_count, dtype=jnp.int32)[None, :]
    )
    scores_new = jnp.where(causal[None], scores_new, -1e30)
    highest = jnp.maximum(jnp.max(scores_old, axis=2), jnp.max(scores_new, axis=2))[:, :, None]
    weights_old = jnp.exp(scores_old - highest)
    weights_new = jnp.where(causal[None], jnp.exp(scores_new - highest), 0.0)
    total = jnp.sum(weights_old, axis=2, keepdims=True) + jnp.sum(
        weights_new, axis=2, keepdims=True
    )
    probs_old = (weights_old / total).astype(jnp.bfloat16)
    probs_new = (weights_new / total).astype(jnp.bfloat16)
    output = jnp.einsum("hqk,khd->qhd", probs_old, values_old, preferred_element_type=jnp.float32)
    output = output + jnp.einsum(
        "hqk,khd->qhd", probs_new, values_new, preferred_element_type=jnp.float32
    )
    return output.reshape(row_count, local_heads * HD).astype(jnp.bfloat16)


def local(
    queries,
    new_keys,
    new_values,
    cache_keys,
    cache_values,
    request_slot,
    tenant_ids,
    out_weight,
    adapter_down,
    adapter_up,
):
    down = reshard_down(adapter_down)
    attended = attention(queries, new_keys, new_values, cache_keys, cache_values, request_slot)
    block, tenants = gather_features(attended, tenant_ids)
    down_count = down.shape[1] // RANK
    up_count = adapter_up.shape[0] // RANK
    part = shrink(block, tenants, down, lax.axis_index("head") * down_count)
    shrunk = sum_everywhere(part).astype(jnp.bfloat16)
    spread = spread_tenants(shrunk, tenants, up_count, lax.axis_index("req") * up_count)
    return scatter_products(block, out_weight, spread, adapter_up)


def solution(mesh):
    placed = (
        P("req", "head"),
        P("req", None),
        P("req", None),
        P("req", None, None),
        P("req", None, None),
        P("req"),
        P("req"),
        P("req", "head"),
        P("head", "req"),
        P("req", "head"),
    )
    return jax.shard_map(
        local, mesh=mesh, in_specs=placed, out_specs=P("req", "head"), check_vma=False
    )
```
